32 devices in a mesh: dom: 8 (over z, x), grid: 4 (over y, core).
Axes of the slice: x: 2, y: 2, z: 4, core: 2. Of those that a mesh axis runs over, the one named last changes fastest.
Arguments:
- adjoint: float32 [4, 6, 1024, 128], P('grid', None, 'dom'), may hold values from -6 to 6
- jac_diag: float32 [4, 6, 6, 1024, 128], P('grid', None, None, 'dom'), may hold values from -6 to 6
- jac_face: float32 [4, 6, 4, 6, 1024, 128], P('grid', None, None, None, 'dom'), may hold values from -3 to 3
- metric: float32 [4, 6, 3, 4, 1024, 128], P('grid', None, None, None, 'dom'), may hold values from -1.5 to 1.5
- node_id: int32 [4, 4, 1024, 128], P('grid', None, 'dom'), may hold values from 0 to 16383
- fringe_cell: int32 [32, 32, 128], P(('dom', 'grid')), may hold values from 0 to 16383
- donor_cell: int32 [32, 32, 128], P(('dom', 'grid')), may hold values from 0 to 16383
- fringe_weight: float32 [32, 32, 128], P(('dom', 'grid')), may hold values from 0.05 to 1
- donor_count: int32 [32, 32], P(('dom', 'grid')), may hold values from 16 to 128, as said below
Outputs:
- product: float32 [4, 6, 1024, 128], P('grid', None, 'dom')
- node_sens: float32 [3, 16384], P(None, ('dom', 'grid'))
The draws below stay inside these ranges and needn't reach their ends.
Inputs may be any that keep to these rules, and one draw needn't show every extreme that they name: The live slots from p to q are slots 0 to donor_count[q, p] - 1; in every draw some receiving device has 128 live slots from every sender.
All inputs are finite; a program needn't handle non-finite values.
Results may differ from the reference program's by a relative error of at most 0.000071.
Values sent between devices are 32-bit elements; how exact they have to be, the bound alone decides.
No kernel may reach another device: no remote copies, remote signals or barrier semaphores. Data moves between devices by JAX's collectives and lax.ppermute only.
A program may use at most 192 MiB of HBM per device.

```python
import math
import jax
import jax.numpy as jnp
from jax import lax

NVAR = 6
BLOCK = 128
FACES = 4
CORNERS = 4
COORDS = 3
ROWS_DEV = 128
CAP = 128
GRIDS = 4
ROWS = 1024
NODES = 16384
N_DOM = 8
DEVICES = 32


def draw_donor_count(key, part):
    key_counts = jax.random.fold_in(key, 11)
    key_full = jax.random.fold_in(key, 23)
    counts = jax.random.randint(key_counts, (DEVICES, DEVICES), CAP // 8, CAP + 1)
    full_row = jax.random.randint(key_full, (), 0, DEVICES)
    row_ids = jnp.arange(DEVICES)[:, None]
    return jnp.where(row_ids == full_row, CAP, counts).astype(jnp.int32)


def set_ends(result, stream_key, smallest, largest):
    extent = result.shape
    index_at = [jax.random.randint(jax.random.fold_in(stream_key, axis), (), 0, extent[axis]) for axis in range(len(extent))]
    result = result.at[tuple(index_at)].set(smallest)
    longest = extent.index(max(extent))
    index_at[longest] = (index_at[longest] + 1) % extent[longest]
    return result.at[tuple(index_at)].set(largest)


def levels(stream_key, extent, cuts, smallest, largest):
    gain = 1.0
    for position, blocks in cuts:
        draws = jax.random.uniform(jax.random.fold_in(jax.random.fold_in(stream_key, 6), position), (blocks,), jnp.float32, smallest / len(cuts), largest / len(cuts))
        gain = gain * jnp.repeat(jnp.exp(draws), extent[position] // blocks).reshape((-1,) + (1,) * (len(extent) - 1 - position))
    return gain


def scatter_about(key, dims, deviation, most, split=(), kind=jnp.bfloat16):
    level = levels(key, dims, split, -0.22, 0.18) if split else 1.0
    array = jax.random.normal(key, dims, jnp.float32) * deviation * level
    return jnp.minimum(jnp.maximum(array, -most), most).astype(kind)


def setup_inputs(seed: int = 0) -> dict:
    streams_of = jax.random.split(jax.random.key(seed), 10)
    return {
        "adjoint": scatter_about(streams_of[0], (GRIDS, NVAR, ROWS, BLOCK), 1.0, 6.0, ((0, 4), (2, 8)), jnp.float32),
        "jac_diag": scatter_about(streams_of[1], (GRIDS, NVAR, NVAR, ROWS, BLOCK), 0.4, 6.0, ((0, 4), (3, 8)), jnp.float32),
        "jac_face": scatter_about(streams_of[2], (GRIDS, NVAR, FACES, NVAR, ROWS, BLOCK), 0.2, 3.0, ((0, 4), (4, 8)), jnp.float32),
        "metric": scatter_about(streams_of[3], (GRIDS, NVAR, COORDS, CORNERS, ROWS, BLOCK), 0.1, 1.5, ((0, 4), (4, 8)), jnp.float32),
        "node_id": set_ends(jax.random.randint(streams_of[4], (GRIDS, CORNERS, ROWS, BLOCK), 0, NODES), jax.random.fold_in(streams_of[4], 1), 0, NODES - 1).astype(jnp.int32),
        "fringe_cell": set_ends(jax.random.randint(streams_of[5], (DEVICES, DEVICES, CAP), 0, ROWS_DEV * BLOCK), jax.random.fold_in(streams_of[5], 1), 0, (ROWS_DEV * BLOCK) - 1).astype(jnp.int32),
        "donor_cell": set_ends(jax.random.randint(streams_of[6], (DEVICES, DEVICES, CAP), 0, ROWS_DEV * BLOCK), jax.random.fold_in(streams_of[6], 1), 0, (ROWS_DEV * BLOCK) - 1).astype(jnp.int32),
        "fringe_weight": jnp.clip(jnp.exp(math.log(1.0) - 2.9957323 * jax.random.uniform(streams_of[7], (DEVICES, DEVICES, CAP), jnp.float32) ** levels(streams_of[7], (DEVICES, DEVICES, CAP), ((0, 32),), -0.2, 0.2)), 0.05, 1.0),
        "donor_count": draw_donor_count(jax.random.fold_in(streams_of[9], 71), 0),
    }


def to_devices(array_field):
    grid_count, var_count = array_field.shape[0], array_field.shape[1]
    by_owner = array_field.reshape(grid_count, var_count, N_DOM, ROWS_DEV * BLOCK)
    return jnp.transpose(by_owner, (2, 0, 1, 3)).reshape(N_DOM * grid_count, var_count, ROWS_DEV * BLOCK)


def from_devices(stacked):
    var_count = stacked.shape[1]
    by_owner = stacked.reshape(N_DOM, GRIDS, var_count, ROWS_DEV * BLOCK)
    return jnp.transpose(by_owner, (1, 2, 0, 3)).reshape(GRIDS, var_count, ROWS, BLOCK)


def pick_slots(values, cell_ids):
    return jnp.take(values, cell_ids, axis=1)


def deposit(values, cell_ids, weights):
    empty = jnp.zeros((NVAR, ROWS_DEV * BLOCK), jnp.float32)
    return empty.at[:, cell_ids].add(-(values * weights[None]))


def reference(adjoint, jac_diag, jac_face, metric, node_id, fringe_cell, donor_cell, fringe_weight, donor_count):
    highest = lax.Precision.HIGHEST
    diagonal_part = jnp.einsum('gijrc,girc->gjrc', jac_diag, adjoint, precision=highest)
    face_terms = jnp.einsum('gifjrc,girc->gfjrc', jac_face, adjoint, precision=highest)
    carried = jnp.pad(face_terms[:, 0, :, 1:, :], ((0, 0), (0, 0), (0, 1), (0, 0)))
    carried = carried + jnp.pad(face_terms[:, 1, :, :-1, :], ((0, 0), (0, 0), (1, 0), (0, 0)))
    carried = carried + jnp.pad(face_terms[:, 2, :, :, 1:], ((0, 0), (0, 0), (0, 0), (0, 1)))
    carried = carried + jnp.pad(face_terms[:, 3, :, :, :-1], ((0, 0), (0, 0), (0, 0), (1, 0)))
    adjoint_dev = to_devices(adjoint)
    payload = jax.vmap(pick_slots)(adjoint_dev, fringe_cell)
    received = jnp.transpose(payload, (2, 1, 0, 3))
    live_slots = jnp.arange(CAP, dtype=jnp.int32)[None, None, :] < donor_count[:, :, None]
    slot_weights = jnp.where(live_slots, fringe_weight, jnp.zeros_like(fringe_weight))
    interp_dev = jax.vmap(deposit)(received, donor_cell, slot_weights)
    product = diagonal_part + carried + from_devices(interp_dev)
    corner_terms = jnp.einsum('gixkrc,girc->xgkrc', metric, adjoint, precision=highest)
    node_sens = jnp.zeros((COORDS, NODES), jnp.float32).at[:, node_id.reshape(-1)].add(corner_terms.reshape(COORDS, -1))
    return product, node_sens
```

```python
import functools

import jax
import jax.numpy as jnp
from jax import lax
from jax.experimental import pallas as pl
from jax.experimental.pallas import tpu as pltpu
from jax.sharding import PartitionSpec as P

NODE_DEV = 512
LANES = 128
SPAN = 256
SPAN_BITS = SPAN.bit_length() - 1
CHUNK = 32
VMEM_BYTES = 48 * 1024 * 1024
LAST_WITH_LAST = (((1,), (1,)), ((), ()))


def ceil_to(value, unit):
    return -(-value // unit) * unit


def sublane_iota(count):
    return lax.broadcasted_iota(jnp.int32, (count, LANES), 0).astype(jnp.bfloat16)


def as_code(index):
    return index.astype(jnp.float32).astype(jnp.bfloat16)


def two_parts(value):
    head = value.astype(jnp.bfloat16)
    tail = (value - head.astype(jnp.float32)).astype(jnp.bfloat16)
    return head, tail


def weighted_sum(load, adj):
    running = load(0) * adj[0]
    for variable in range(1, len(adj)):
        running = running + load(variable) * adj[variable]
    return running


def gather_and_nodes(
    place, adj_ref, metric_ref, node_ref, fringe_ref, first_ref, last_ref, out_ref, totals, split_adj
):
    step = pl.program_id(0)
    steps = pl.num_programs(0)
    variables, row_count, width = adj_ref.shape
    coords, corners, rows = metric_ref.shape[1:4]
    peers = out_ref.shape[0]
    spans = totals.shape[0] // (2 * coords)
    span_rows = SPAN // width
    node_rows = coords * NODE_DEV // width
    payload_at = node_rows
    halo_at = node_rows + variables
    zero = jnp.zeros((), jnp.bfloat16)
    one = jnp.ones((), jnp.bfloat16)

    @pl.when(step == 0)
    def _():
        head, tail = two_parts(adj_ref[...].reshape(variables * row_count, width))
        split_adj[:, :width] = head
        split_adj[:, width:] = tail
        out_ref[:, halo_at:, :] = jnp.zeros((peers, out_ref.shape[1] - halo_at, width), jnp.float32)
        top = [adj_ref[i, : first_ref.shape[3], :] for i in range(variables)]
        bottom = [adj_ref[i, row_count - last_ref.shape[3] :, :] for i in range(variables)]
        for j in range(variables):
            face_down = weighted_sum(lambda i: first_ref[i, 0, j], top)
            face_up = weighted_sum(lambda i: last_ref[i, 0, j], bottom)

            @pl.when(place[0] >= 0)
            def _():
                out_ref[place[0], pl.ds(halo_at + j, 1), :] = face_down[:1]

            @pl.when(place[1] >= 0)
            def _():
                out_ref[place[1], pl.ds(halo_at + j, 1), :] = face_up[-1:]

    row_at = pl.multiple_of(step * rows, rows)
    adj = [adj_ref[i, pl.ds(row_at, rows), :] for i in range(variables)]
    span_code = sublane_iota(spans)
    place_code = sublane_iota(SPAN)
    left = []
    right = []
    for corner in range(corners):
        ids = node_ref[corner]
        span = ids >> SPAN_BITS
        owner_rows = NODE_DEV // SPAN
        span = (span & (owner_rows - 1)) * peers + (span >> (owner_rows.bit_length() - 1))
        span = as_code(span)
        inside = as_code(ids & (SPAN - 1))
        values = []
        for x in range(coords):
            values.extend(two_parts(weighted_sum(lambda i: metric_ref[i, x, corner], adj)))
        for r in range(rows):
            hit = span_code == span[r : r + 1]
            left.append(jnp.concatenate([jnp.where(hit, v[r : r + 1], zero) for v in values], axis=0))
            right.append(jnp.where(place_code == inside[r : r + 1], one, zero))
    added = lax.dot_general(
        jnp.concatenate(left, axis=1),
        jnp.concatenate(right, axis=1),
        LAST_WITH_LAST,
        preferred_element_type=jnp.float32,
    )
    totals[...] = jnp.where(step == 0, 0.0, totals[...]) + added

    share = fringe_ref.shape[0]
    row_code = sublane_iota(row_count)
    for q in range(share):
        cell = fringe_ref[pl.ds(q, 1), :]
        column = as_code(cell & (width - 1))
        row = cell >> (width.bit_length() - 1)
        pick = jnp.where(sublane_iota(width) == column, one, zero)
        found = jnp.dot(
            split_adj[...],
            jnp.concatenate([pick, pick], axis=0),
            preferred_element_type=jnp.float32,
        )
        mine = lax.broadcasted_iota(jnp.int32, (row_count, width), 0) == row
        for i in range(variables):
            part = found[i * row_count : (i + 1) * row_count]
            line = jnp.sum(jnp.where(mine, part, 0.0), axis=0, keepdims=True)
            out_ref[step * share + q, pl.ds(payload_at + i, 1), :] = line

    @pl.when(step == steps - 1)
    def _():
        for x in range(coords):
            both = totals[pl.ds(2 * x * spans, spans), :] + totals[pl.ds((2 * x + 1) * spans, spans), :]
            for part in range(NODE_DEV // SPAN):
                for half in range(span_rows):
                    at = (x * (NODE_DEV // SPAN) + part) * span_rows + half
                    out_ref[:, at, :] = both[part * peers : (part + 1) * peers, half * width : (half + 1) * width]


def jacobian(adj_ref, diag_ref, face_ref, out_ref, carry):
    step = pl.program_id(0)
    variables, rows, width = adj_ref.shape
    row_at = pl.multiple_of(step * rows, rows)
    adj = [adj_ref[i] for i in range(variables)]
    row_ids = lax.broadcasted_iota(jnp.int32, (rows, width), 0)
    lane_ids = lax.broadcasted_iota(jnp.int32, (rows, width), 1)

    @pl.when(step == 0)
    def _():
        carry[...] = jnp.zeros_like(carry)

    for j in range(variables):
        total = weighted_sum(lambda i: diag_ref[i, j], adj)
        faces = [weighted_sum(lambda i: face_ref[i, f, j], adj) for f in range(4)]
        below = pltpu.roll(faces[0], rows - 1, 0)
        total = total + jnp.where(row_ids < rows - 1, below, 0.0)
        above = pltpu.roll(faces[1], 1, 0)
        total = total + jnp.where(row_ids > 0, above, carry[pl.ds(j, 1), :])
        right = pltpu.roll(faces[2], width - 1, 1)
        total = total + jnp.where(lane_ids < width - 1, right, 0.0)
        left = pltpu.roll(faces[3], 1, 1)
        total = total + jnp.where(lane_ids > 0, left, 0.0)
        out_ref[j, pl.ds(row_at, rows), :] = total
        carry[pl.ds(j, 1), :] = faces[1][rows - 1 :]

        @pl.when(step > 0)
        def _():
            out_ref[j, pl.ds(row_at - 1, 1), :] += faces[0][:1]


def finish(place, count_ref, recv_ref, cell_ref, weight_ref, base_ref, out_ref, sens_ref):
    variables, row_count, width = base_ref.shape
    peers = recv_ref.shape[0]
    coords = sens_ref.shape[0]
    node_rows = coords * NODE_DEV // width
    payload_at = node_rows
    halo_at = node_rows + variables
    spans = row_count * width // SPAN
    span_rows = SPAN // width
    zero = jnp.zeros((), jnp.bfloat16)
    one = jnp.ones((), jnp.bfloat16)

    sums = jnp.sum(recv_ref[:, :node_rows, :], axis=0)
    per_coord = node_rows // coords
    for x in range(coords):
        for part in range(per_coord):
            at = x * per_coord + part
            sens_ref[pl.ds(x, 1), pl.ds(part * width, width)] = sums[at : at + 1]

    span_code = sublane_iota(spans)
    place_code = sublane_iota(SPAN)
    slot = lax.broadcasted_iota(jnp.int32, (1, width), 1)
    chunk = min(CHUNK, peers)
    for start in range(0, peers, chunk):
        left = []
        right = []
        for q in range(start, start + chunk):
            weight = jnp.where(slot < count_ref[0, q], weight_ref[pl.ds(q, 1), :], 0.0)
            values = two_parts(-(recv_ref[q, pl.ds(payload_at, variables), :] * weight))
            cell = cell_ref[pl.ds(q, 1), :]
            hit = span_code == as_code(cell >> SPAN_BITS)
            left.append(
                jnp.concatenate(
                    [jnp.where(hit, v[i : i + 1], zero) for i in range(variables) for v in values], axis=0
                )
            )
            right.append(jnp.where(place_code == as_code(cell & (SPAN - 1)), one, zero))
        added = lax.dot_general(
            jnp.concatenate(left, axis=1),
            jnp.concatenate(right, axis=1),
            LAST_WITH_LAST,
            preferred_element_type=jnp.float32,
        )
        source = base_ref if start == 0 else out_ref
        for i in range(variables):
            both = added[2 * i * spans : (2 * i + 1) * spans] + added[(2 * i + 1) * spans : (2 * i + 2) * spans]
            for half in range(span_rows):
                where = pl.ds(half, spans, stride=span_rows)
                out_ref[i, where, :] = source[i, where, :] + both[:, half * width : (half + 1) * width]

    @pl.when(place[0] >= 0)
    def _():
        out_ref[:, :1, :] += recv_ref[place[0], pl.ds(halo_at, variables), :].reshape(variables, 1, width)

    @pl.when(place[1] >= 0)
    def _():
        out_ref[:, row_count - 1 :, :] += recv_ref[place[1], pl.ds(halo_at, variables), :].reshape(
            variables, 1, width
        )


def local(
    adjoint,
    jac_diag,
    jac_face,
    metric,
    node_id,
    fringe_cell,
    donor_cell,
    fringe_weight,
    donor_count,
):
    adj, diag, face, met = adjoint[0], jac_diag[0], jac_face[0], metric[0]
    variables, row_count, width = adj.shape
    faces = face.shape[1]
    coords, corners = met.shape[1:3]
    doms, grids = lax.axis_size("dom"), lax.axis_size("grid")
    peers = doms * grids
    node_rows = coords * NODE_DEV // width
    used = node_rows + 2 * variables
    sent_rows = ceil_to(used, 8)
    spans = peers * NODE_DEV // SPAN
    here, lane = lax.axis_index("dom"), lax.axis_index("grid")
    before = jnp.where(here > 0, (here - 1) * grids + lane, -1)
    after = jnp.where(here < doms - 1, (here + 1) * grids + lane, -1)
    place = jnp.stack([before, after]).astype(jnp.int32)
    params = pltpu.CompilerParams(vmem_limit_bytes=VMEM_BYTES)

    rows = 16 if spans <= 64 else 8
    steps = row_count // rows
    share = peers // steps
    edge = 8
    sent = pl.pallas_call(
        gather_and_nodes,
        grid_spec=pltpu.PrefetchScalarGridSpec(
            num_scalar_prefetch=1,
            grid=(steps,),
            in_specs=[
                pl.BlockSpec((variables, row_count, width), lambda s, p: (0, 0, 0)),
                pl.BlockSpec((variables, coords, corners, rows, width), lambda s, p: (0, 0, 0, s, 0)),
                pl.BlockSpec((corners, rows, width), lambda s, p: (0, s, 0)),
                pl.BlockSpec((pl.Squeezed(), share, width), lambda s, p: (s, 0, 0)),
                pl.BlockSpec((variables, 1, variables, edge, width), lambda s, p: (0, 0, 0, 0, 0)),
                pl.BlockSpec(
                    (variables, 1, variables, edge, width), lambda s, p: (0, 1, 0, row_count // edge - 1, 0)
                ),
            ],
            out_specs=pl.BlockSpec((peers, sent_rows, width), lambda s, p: (0, 0, 0)),
            scratch_shapes=[
                pltpu.VMEM((2 * coords * spans, SPAN), jnp.float32),
                pltpu.VMEM((variables * row_count, 2 * width), jnp.bfloat16),
            ],
        ),
        out_shape=jax.ShapeDtypeStruct((peers, sent_rows, width), jnp.float32),
        compiler_params=params,
        cost_estimate=pl.CostEstimate(
            flops=4 * coords * spans * SPAN * corners * row_count * width,
            bytes_accessed=met.size * 4,
            transcendentals=0,
        ),
        name="gather_and_nodes",
    )(place, adj, met, node_id[0], fringe_cell[0].reshape(steps, share, width), face, face)

    received = lax.all_to_all(sent, ("dom", "grid"), split_axis=0, concat_axis=0, tiled=True)

    jac_rows = 16
    base = pl.pallas_call(
        jacobian,
        grid=(row_count // jac_rows,),
        in_specs=[
            pl.BlockSpec((variables, jac_rows, width), lambda s: (0, s, 0)),
            pl.BlockSpec((variables, variables, jac_rows, width), lambda s: (0, 0, s, 0)),
            pl.BlockSpec((variables, faces, variables, jac_rows, width), lambda s: (0, 0, 0, s, 0)),
        ],
        out_specs=pl.BlockSpec((variables, row_count, width), lambda s: (0, 0, 0)),
        out_shape=jax.ShapeDtypeStruct((variables, row_count, width), jnp.float32),
        scratch_shapes=[pltpu.VMEM((8, width), jnp.float32)],
        compiler_params=params,
        cost_estimate=pl.CostEstimate(
            flops=2 * (diag.size + face.size), bytes_accessed=4 * (diag.size + face.size), transcendentals=0
        ),
        name="jacobian",
    )(adj, diag, face)

    vmem = pl.BlockSpec(memory_space=pltpu.VMEM)
    smem = pl.BlockSpec(memory_space=pltpu.SMEM)
    product, node_sens = pl.pallas_call(
        finish,
        in_specs=[smem, smem, vmem, vmem, vmem, vmem],
        out_specs=[vmem, vmem],
        out_shape=[
            jax.ShapeDtypeStruct((variables, row_count, width), jnp.float32),
            jax.ShapeDtypeStruct((coords, NODE_DEV), jnp.float32),
        ],
        compiler_params=params,
        name="finish",
    )(place, donor_count, received, donor_cell[0], fringe_weight[0], base)
    return (product[None], node_sens)


def solution(mesh):
    in_specs = (
        P("grid", None, "dom", None),
        P("grid", None, None, "dom", None),
        P("grid", None, None, None, "dom", None),
        P("grid", None, None, None, "dom", None),
        P("grid", None, "dom", None),
        P(("dom", "grid"), None, None),
        P(("dom", "grid"), None, None),
        P(("dom", "grid"), None, None),
        P(("dom", "grid"), None),
    )
    out_specs = (P("grid", None, "dom", None), P(None, ("dom", "grid")))
    return jax.shard_map(local, mesh=mesh, in_specs=in_specs, out_specs=out_specs, check_vma=False)
```

```python
import functools

import jax
import jax.numpy as jnp
from jax import lax
from jax.experimental import pallas as pl
from jax.experimental.pallas import tpu as pltpu
from jax.sharding import PartitionSpec as P

NODE_DEV = 512
LANES = 128
SPAN = 256
SPAN_BITS = SPAN.bit_length() - 1
CHUNK = 32
VMEM_BYTES = 62 * 1024 * 1024
LAST_WITH_LAST = (((1,), (1,)), ((), ()))


def ceil_to(value, unit):
    return -(-value // unit) * unit


def sublane_iota(count):
    return lax.broadcasted_iota(jnp.int32, (count, LANES), 0).astype(jnp.bfloat16)


def as_code(index):
    return index.astype(jnp.float32).astype(jnp.bfloat16)


def two_parts(value):
    head = value.astype(jnp.bfloat16)
    tail = (value - head.astype(jnp.float32)).astype(jnp.bfloat16)
    return head, tail


def weighted_sum(load, adj):
    running = load(0) * adj[0]
    for variable in range(1, len(adj)):
        running = running + load(variable) * adj[variable]
    return running


def gather_and_nodes(
    place, adj_ref, metric_ref, node_ref, fringe_ref, first_ref, last_ref, out_ref, totals, split_adj
):
    step = pl.program_id(0)
    steps = pl.num_programs(0)
    variables, row_count, width = adj_ref.shape
    coords, corners, rows = metric_ref.shape[1:4]
    peers = out_ref.shape[0]
    spans = totals.shape[0] // (2 * coords)
    span_rows = SPAN // width
    node_rows = coords * NODE_DEV // width
    payload_at = node_rows
    halo_at = node_rows + variables
    zero = jnp.zeros((), jnp.bfloat16)
    one = jnp.ones((), jnp.bfloat16)

    @pl.when(step == 0)
    def _():
        head, tail = two_parts(adj_ref[...].reshape(variables * row_count, width))
        split_adj[:, :width] = head
        split_adj[:, width:] = tail
        out_ref[:, halo_at:, :] = jnp.zeros((peers, out_ref.shape[1] - halo_at, width), jnp.float32)
        top = [adj_ref[i, : first_ref.shape[3], :] for i in range(variables)]
        bottom = [adj_ref[i, row_count - last_ref.shape[3] :, :] for i in range(variables)]
        for j in range(variables):
            face_down = weighted_sum(lambda i: first_ref[i, 0, j], top)
            face_up = weighted_sum(lambda i: last_ref[i, 0, j], bottom)

            @pl.when(place[0] >= 0)
            def _():
                out_ref[place[0], pl.ds(halo_at + j, 1), :] = face_down[:1]

            @pl.when(place[1] >= 0)
            def _():
                out_ref[place[1], pl.ds(halo_at + j, 1), :] = face_up[-1:]

    row_at = pl.multiple_of(step * rows, rows)
    adj = [adj_ref[i, pl.ds(row_at, rows), :] for i in range(variables)]
    span_code = sublane_iota(spans)
    place_code = sublane_iota(SPAN)
    left = []
    right = []
    for corner in range(corners):
        ids = node_ref[corner]
        span = ids >> SPAN_BITS
        owner_rows = NODE_DEV // SPAN
        span = (span & (owner_rows - 1)) * peers + (span >> (owner_rows.bit_length() - 1))
        span = as_code(span)
        inside = as_code(ids & (SPAN - 1))
        values = []
        for x in range(coords):
            values.extend(two_parts(weighted_sum(lambda i: metric_ref[i, x, corner], adj)))
        for r in range(rows):
            hit = span_code == span[r : r + 1]
            left.append(jnp.concatenate([jnp.where(hit, v[r : r + 1], zero) for v in values], axis=0))
            right.append(jnp.where(place_code == inside[r : r + 1], one, zero))
    added = lax.dot_general(
        jnp.concatenate(left, axis=1),
        jnp.concatenate(right, axis=1),
        LAST_WITH_LAST,
        preferred_element_type=jnp.float32,
    )
    totals[...] = jnp.where(step == 0, 0.0, totals[...]) + added

    share = fringe_ref.shape[0]
    row_code = sublane_iota(row_count)
    for q in range(share):
        cell = fringe_ref[pl.ds(q, 1), :]
        column = as_code(cell & (width - 1))
        row = cell >> (width.bit_length() - 1)
        pick = jnp.where(sublane_iota(width) == column, one, zero)
        found = jnp.dot(
            split_adj[...],
            jnp.concatenate([pick, pick], axis=0),
            preferred_element_type=jnp.float32,
        )
        mine = lax.broadcasted_iota(jnp.int32, (row_count, width), 0) == row
        for i in range(variables):
            part = found[i * row_count : (i + 1) * row_count]
            line = jnp.sum(jnp.where(mine, part, 0.0), axis=0, keepdims=True)
            out_ref[step * share + q, pl.ds(payload_at + i, 1), :] = line

    @pl.when(step == steps - 1)
    def _():
        for x in range(coords):
            both = totals[pl.ds(2 * x * spans, spans), :] + totals[pl.ds((2 * x + 1) * spans, spans), :]
            for part in range(NODE_DEV // SPAN):
                for half in range(span_rows):
                    at = (x * (NODE_DEV // SPAN) + part) * span_rows + half
                    out_ref[:, at, :] = both[part * peers : (part + 1) * peers, half * width : (half + 1) * width]


def jacobian(adj_ref, diag_ref, face_ref, out_ref, carry):
    step = pl.program_id(0)
    variables, rows, width = adj_ref.shape
    row_at = pl.multiple_of(step * rows, rows)
    adj = [adj_ref[i] for i in range(variables)]
    row_ids = lax.broadcasted_iota(jnp.int32, (rows, width), 0)
    lane_ids = lax.broadcasted_iota(jnp.int32, (rows, width), 1)

    @pl.when(step == 0)
    def _():
        carry[...] = jnp.zeros_like(carry)

    for j in range(variables):
        total = weighted_sum(lambda i: diag_ref[i, j], adj)
        faces = [weighted_sum(lambda i: face_ref[i, f, j], adj) for f in range(4)]
        below = pltpu.roll(faces[0], rows - 1, 0)
        total = total + jnp.where(row_ids < rows - 1, below, 0.0)
        above = pltpu.roll(faces[1], 1, 0)
        total = total + jnp.where(row_ids > 0, above, carry[pl.ds(j, 1), :])
        right = pltpu.roll(faces[2], width - 1, 1)
        total = total + jnp.where(lane_ids < width - 1, right, 0.0)
        left = pltpu.roll(faces[3], 1, 1)
        total = total + jnp.where(lane_ids > 0, left, 0.0)
        out_ref[j, pl.ds(row_at, rows), :] = total
        carry[pl.ds(j, 1), :] = faces[1][rows - 1 :]

        @pl.when(step > 0)
        def _():
            out_ref[j, pl.ds(row_at - 1, 1), :] += faces[0][:1]


def finish(place, count_ref, recv_ref, cell_ref, weight_ref, base_ref, out_ref, sens_ref):
    variables, row_count, width = base_ref.shape
    peers = recv_ref.shape[0]
    coords = sens_ref.shape[0]
    node_rows = coords * NODE_DEV // width
    payload_at = node_rows
    halo_at = node_rows + variables
    spans = row_count * width // SPAN
    span_rows = SPAN // width
    zero = jnp.zeros((), jnp.bfloat16)
    one = jnp.ones((), jnp.bfloat16)

    sums = jnp.sum(recv_ref[:, :node_rows, :], axis=0)
    per_coord = node_rows // coords
    for x in range(coords):
        for part in range(per_coord):
            at = x * per_coord + part
            sens_ref[pl.ds(x, 1), pl.ds(part * width, width)] = sums[at : at + 1]

    span_code = sublane_iota(spans)
    place_code = sublane_iota(SPAN)
    slot = lax.broadcasted_iota(jnp.int32, (1, width), 1)
    chunk = min(CHUNK, peers)
    for start in range(0, peers, chunk):
        left = []
        right = []
        for q in range(start, start + chunk):
            weight = jnp.where(slot < count_ref[0, q], weight_ref[pl.ds(q, 1), :], 0.0)
            values = two_parts(-(recv_ref[q, pl.ds(payload_at, variables), :] * weight))
            cell = cell_ref[pl.ds(q, 1), :]
            hit = span_code == as_code(cell >> SPAN_BITS)
            left.append(
                jnp.concatenate(
                    [jnp.where(hit, v[i : i + 1], zero) for i in range(variables) for v in values], axis=0
                )
            )
            right.append(jnp.where(place_code == as_code(cell & (SPAN - 1)), one, zero))
        added = lax.dot_general(
            jnp.concatenate(left, axis=1),
            jnp.concatenate(right, axis=1),
            LAST_WITH_LAST,
            preferred_element_type=jnp.float32,
        )
        source = base_ref if start == 0 else out_ref
        for i in range(variables):
            both = added[2 * i * spans : (2 * i + 1) * spans] + added[(2 * i + 1) * spans : (2 * i + 2) * spans]
            for half in range(span_rows):
                where = pl.ds(half, spans, stride=span_rows)
                out_ref[i, where, :] = source[i, where, :] + both[:, half * width : (half + 1) * width]

    @pl.when(place[0] >= 0)
    def _():
        out_ref[:, :1, :] += recv_ref[place[0], pl.ds(halo_at, variables), :].reshape(variables, 1, width)

    @pl.when(place[1] >= 0)
    def _():
        out_ref[:, row_count - 1 :, :] += recv_ref[place[1], pl.ds(halo_at, variables), :].reshape(
            variables, 1, width
        )


def local(
    adjoint,
    jac_diag,
    jac_face,
    metric,
    node_id,
    fringe_cell,
    donor_cell,
    fringe_weight,
    donor_count,
):
    adj, diag, face, met = adjoint[0], jac_diag[0], jac_face[0], metric[0]
    variables, row_count, width = adj.shape
    faces = face.shape[1]
    coords, corners = met.shape[1:3]
    doms, grids = lax.axis_size("dom"), lax.axis_size("grid")
    peers = doms * grids
    node_rows = coords * NODE_DEV // width
    used = node_rows + 2 * variables
    sent_rows = ceil_to(used, 8)
    spans = peers * NODE_DEV // SPAN
    here, lane = lax.axis_index("dom"), lax.axis_index("grid")
    before = jnp.where(here > 0, (here - 1) * grids + lane, -1)
    after = jnp.where(here < doms - 1, (here + 1) * grids + lane, -1)
    place = jnp.stack([before, after]).astype(jnp.int32)
    params = pltpu.CompilerParams(vmem_limit_bytes=VMEM_BYTES)

    rows = 16 if spans <= 64 else 8
    steps = row_count // rows
    share = peers // steps
    edge = 8
    sent = pl.pallas_call(
        gather_and_nodes,
        grid_spec=pltpu.PrefetchScalarGridSpec(
            num_scalar_prefetch=1,
            grid=(steps,),
            in_specs=[
                pl.BlockSpec((variables, row_count, width), lambda s, p: (0, 0, 0)),
                pl.BlockSpec((variables, coords, corners, rows, width), lambda s, p: (0, 0, 0, s, 0)),
                pl.BlockSpec((corners, rows, width), lambda s, p: (0, s, 0)),
                pl.BlockSpec((pl.Squeezed(), share, width), lambda s, p: (s, 0, 0)),
                pl.BlockSpec((variables, 1, variables, edge, width), lambda s, p: (0, 0, 0, 0, 0)),
                pl.BlockSpec(
                    (variables, 1, variables, edge, width), lambda s, p: (0, 1, 0, row_count // edge - 1, 0)
                ),
            ],
            out_specs=pl.BlockSpec((peers, sent_rows, width), lambda s, p: (0, 0, 0)),
            scratch_shapes=[
                pltpu.VMEM((2 * coords * spans, SPAN), jnp.float32),
                pltpu.VMEM((variables * row_count, 2 * width), jnp.bfloat16),
            ],
        ),
        out_shape=jax.ShapeDtypeStruct((peers, sent_rows, width), jnp.float32),
        compiler_params=params,
        cost_estimate=pl.CostEstimate(
            flops=4 * coords * spans * SPAN * corners * row_count * width,
            bytes_accessed=met.size * 4,
            transcendentals=0,
        ),
        name="gather_and_nodes",
    )(place, adj, met, node_id[0], fringe_cell[0].reshape(steps, share, width), face, face)

    received = lax.all_to_all(sent, ("dom", "grid"), split_axis=0, concat_axis=0, tiled=True)

    jac_rows = 16
    base = pl.pallas_call(
        jacobian,
        grid=(row_count // jac_rows,),
        in_specs=[
            pl.BlockSpec((variables, jac_rows, width), lambda s: (0, s, 0)),
            pl.BlockSpec((variables, variables, jac_rows, width), lambda s: (0, 0, s, 0)),
            pl.BlockSpec((variables, faces, variables, jac_rows, width), lambda s: (0, 0, 0, s, 0)),
        ],
        out_specs=pl.BlockSpec((variables, row_count, width), lambda s: (0, 0, 0)),
        out_shape=jax.ShapeDtypeStruct((variables, row_count, width), jnp.float32),
        scratch_shapes=[pltpu.VMEM((8, width), jnp.float32)],
        compiler_params=params,
        cost_estimate=pl.CostEstimate(
            flops=2 * (diag.size + face.size), bytes_accessed=4 * (diag.size + face.size), transcendentals=0
        ),
        name="jacobian",
    )(adj, diag, face)

    vmem = pl.BlockSpec(memory_space=pltpu.VMEM)
    smem = pl.BlockSpec(memory_space=pltpu.SMEM)
    product, node_sens = pl.pallas_call(
        finish,
        in_specs=[smem, smem, vmem, vmem, vmem, vmem],
        out_specs=[vmem, vmem],
        out_shape=[
            jax.ShapeDtypeStruct((variables, row_count, width), jnp.float32),
            jax.ShapeDtypeStruct((coords, NODE_DEV), jnp.float32),
        ],
        compiler_params=params,
        name="finish",
    )(place, donor_count, received, donor_cell[0], fringe_weight[0], base)
    return (product[None], node_sens)


def solution(mesh):
    in_specs = (
        P("grid", None, "dom", None),
        P("grid", None, None, "dom", None),
        P("grid", None, None, None, "dom", None),
        P("grid", None, None, None, "dom", None),
        P("grid", None, "dom", None),
        P(("dom", "grid"), None, None),
        P(("dom", "grid"), None, None),
        P(("dom", "grid"), None, None),
        P(("dom", "grid"), None),
    )
    out_specs = (P("grid", None, "dom", None), P(None, ("dom", "grid")))
    return jax.shard_map(local, mesh=mesh, in_specs=in_specs, out_specs=out_specs, check_vma=False)
```

```python
import functools

import jax
import jax.numpy as jnp
from jax import lax
from jax.experimental import pallas as pl
from jax.experimental.pallas import tpu as pltpu
from jax.sharding import PartitionSpec as P

NODE_DEV = 512
LANES = 128
SPAN = 256
SPAN_BITS = SPAN.bit_length() - 1
CHUNK = 32
VMEM_BYTES = 62 * 1024 * 1024
LAST_WITH_LAST = (((1,), (1,)), ((), ()))


def neighbours(dom="dom", grid="grid"):
    here, lane = lax.axis_index(dom), lax.axis_index(grid)
    doms, grids = lax.axis_size(dom), lax.axis_size(grid)
    before, after = (here - 1) * grids + lane, (here + 1) * grids + lane
    return here > 0, before, here < doms - 1, after


def ceil_to(value, unit):
    return -(-value // unit) * unit


def sublane_iota(count):
    return lax.broadcasted_iota(jnp.int32, (count, LANES), 0).astype(jnp.bfloat16)


def as_code(index):
    return index.astype(jnp.float32).astype(jnp.bfloat16)


def two_parts(value):
    head = value.astype(jnp.bfloat16)
    tail = (value - head.astype(jnp.float32)).astype(jnp.bfloat16)
    return head, tail


def weighted_sum(load, adj):
    running = load(0) * adj[0]
    for variable in range(1, len(adj)):
        running = running + load(variable) * adj[variable]
    return running


def gather_and_nodes(
    adj_ref, metric_ref, node_ref, fringe_ref, first_ref, last_ref, out_ref, totals, split_adj
):
    step = pl.program_id(0)
    steps = pl.num_programs(0)
    variables, row_count, width = adj_ref.shape
    coords, corners, rows = metric_ref.shape[1:4]
    peers = out_ref.shape[0]
    spans = totals.shape[0] // (2 * coords)
    span_rows = SPAN // width
    node_rows = coords * NODE_DEV // width
    payload_at = node_rows
    halo_at = node_rows + variables
    zero = jnp.zeros((), jnp.bfloat16)
    one = jnp.ones((), jnp.bfloat16)

    @pl.when(step == 0)
    def _():
        head, tail = two_parts(adj_ref[...].reshape(variables * row_count, width))
        split_adj[:, :width] = head
        split_adj[:, width:] = tail
        out_ref[:, halo_at:, :] = jnp.zeros((peers, out_ref.shape[1] - halo_at, width), jnp.float32)
        top = [adj_ref[i, : first_ref.shape[3], :] for i in range(variables)]
        bottom = [adj_ref[i, row_count - last_ref.shape[3] :, :] for i in range(variables)]
        has_before, before, has_after, after = neighbours()
        for j in range(variables):
            face_down = weighted_sum(lambda i: first_ref[i, 0, j], top)
            face_up = weighted_sum(lambda i: last_ref[i, 0, j], bottom)

            @pl.when(has_before)
            def _():
                out_ref[before, pl.ds(halo_at + j, 1), :] = face_down[:1]

            @pl.when(has_after)
            def _():
                out_ref[after, pl.ds(halo_at + j, 1), :] = face_up[-1:]

    row_at = pl.multiple_of(step * rows, rows)
    adj = [adj_ref[i, pl.ds(row_at, rows), :] for i in range(variables)]
    span_code = sublane_iota(spans)
    place_code = sublane_iota(SPAN)
    left = []
    right = []
    for corner in range(corners):
        ids = node_ref[corner]
        span = ids >> SPAN_BITS
        owner_rows = NODE_DEV // SPAN
        span = (span & (owner_rows - 1)) * peers + (span >> (owner_rows.bit_length() - 1))
        span = as_code(span)
        inside = as_code(ids & (SPAN - 1))
        values = []
        for x in range(coords):
            values.extend(two_parts(weighted_sum(lambda i: metric_ref[i, x, corner], adj)))
        for r in range(rows):
            hit = span_code == span[r : r + 1]
            left.append(jnp.concatenate([jnp.where(hit, v[r : r + 1], zero) for v in values], axis=0))
            right.append(jnp.where(place_code == inside[r : r + 1], one, zero))
    added = lax.dot_general(
        jnp.concatenate(left, axis=1),
        jnp.concatenate(right, axis=1),
        LAST_WITH_LAST,
        preferred_element_type=jnp.float32,
    )
    totals[...] = jnp.where(step == 0, 0.0, totals[...]) + added

    share = fringe_ref.shape[0]
    column_code = sublane_iota(width)
    row_ids = lax.broadcasted_iota(jnp.int32, (row_count, width), 0)
    picks = []
    for q in range(share):
        pick = jnp.where(column_code == as_code(fringe_ref[pl.ds(q, 1), :] & (width - 1)), one, zero)
        picks.append(jnp.concatenate([pick, pick], axis=0))
    found = jnp.dot(split_adj[...], jnp.concatenate(picks, axis=1), preferred_element_type=jnp.float32)
    for q in range(share):
        mine = row_ids == fringe_ref[pl.ds(q, 1), :] >> (width.bit_length() - 1)
        for i in range(variables):
            part = found[i * row_count : (i + 1) * row_count, q * width : (q + 1) * width]
            line = jnp.sum(jnp.where(mine, part, 0.0), axis=0, keepdims=True)
            out_ref[step * share + q, pl.ds(payload_at + i, 1), :] = line

    @pl.when(step == steps - 1)
    def _():
        for x in range(coords):
            both = totals[pl.ds(2 * x * spans, spans), :] + totals[pl.ds((2 * x + 1) * spans, spans), :]
            for part in range(NODE_DEV // SPAN):
                for half in range(span_rows):
                    at = (x * (NODE_DEV // SPAN) + part) * span_rows + half
                    out_ref[:, at, :] = both[part * peers : (part + 1) * peers, half * width : (half + 1) * width]


def jacobian(count_ref, weight_ref, adj_ref, diag_ref, face_ref, out_ref, minus_ref):
    variables, row_count, width = adj_ref.shape
    peers = weight_ref.shape[0]

    @pl.when(pl.program_id(0) == 0)
    def _():
        slot = lax.broadcasted_iota(jnp.int32, (1, width), 1)
        for q in range(peers):
            minus_ref[pl.ds(q, 1), :] = jnp.where(slot < count_ref[0, q], -weight_ref[pl.ds(q, 1), :], 0.0)

    adj = [adj_ref[i] for i in range(variables)]
    row_ids = lax.broadcasted_iota(jnp.int32, (row_count, width), 0)
    lane_ids = lax.broadcasted_iota(jnp.int32, (row_count, width), 1)
    total = weighted_sum(lambda i: diag_ref[i], adj)
    faces = [weighted_sum(lambda i: face_ref[i, f], adj) for f in range(4)]
    below = pltpu.roll(faces[0], row_count - 1, 0)
    total = total + jnp.where(row_ids < row_count - 1, below, 0.0)
    above = pltpu.roll(faces[1], 1, 0)
    total = total + jnp.where(row_ids > 0, above, 0.0)
    right = pltpu.roll(faces[2], width - 1, 1)
    total = total + jnp.where(lane_ids < width - 1, right, 0.0)
    left = pltpu.roll(faces[3], 1, 1)
    out_ref[...] = total + jnp.where(lane_ids > 0, left, 0.0)


def finish(recv_ref, cell_ref, weight_ref, base_ref, out_ref, sens_ref):
    variables, row_count, width = base_ref.shape
    peers = recv_ref.shape[0]
    coords = sens_ref.shape[0]
    node_rows = coords * NODE_DEV // width
    payload_at = node_rows
    halo_at = node_rows + variables
    spans = row_count * width // SPAN
    span_rows = SPAN // width
    zero = jnp.zeros((), jnp.bfloat16)
    one = jnp.ones((), jnp.bfloat16)

    sums = jnp.sum(recv_ref[:, :node_rows, :], axis=0)
    per_coord = node_rows // coords
    for x in range(coords):
        for part in range(per_coord):
            at = x * per_coord + part
            sens_ref[pl.ds(x, 1), pl.ds(part * width, width)] = sums[at : at + 1]

    span_code = sublane_iota(spans)
    place_code = sublane_iota(SPAN)
    chunk = min(CHUNK, peers)
    for start in range(0, peers, chunk):
        left = []
        right = []
        for q in range(start, start + chunk):
            weight = weight_ref[pl.ds(q, 1), :]
            values = two_parts(recv_ref[q, pl.ds(payload_at, variables), :] * weight)
            cell = cell_ref[pl.ds(q, 1), :]
            hit = span_code == as_code(cell >> SPAN_BITS)
            left.append(
                jnp.concatenate(
                    [jnp.where(hit, v[i : i + 1], zero) for i in range(variables) for v in values], axis=0
                )
            )
            right.append(jnp.where(place_code == as_code(cell & (SPAN - 1)), one, zero))
        added = lax.dot_general(
            jnp.concatenate(left, axis=1),
            jnp.concatenate(right, axis=1),
            LAST_WITH_LAST,
            preferred_element_type=jnp.float32,
        )
        source = base_ref if start == 0 else out_ref
        for i in range(variables):
            both = added[2 * i * spans : (2 * i + 1) * spans] + added[(2 * i + 1) * spans : (2 * i + 2) * spans]
            for half in range(span_rows):
                where = pl.ds(half, spans, stride=span_rows)
                out_ref[i, where, :] = source[i, where, :] + both[:, half * width : (half + 1) * width]

    has_before, before, has_after, after = neighbours()

    @pl.when(has_before)
    def _():
        out_ref[:, :1, :] += recv_ref[before, pl.ds(halo_at, variables), :].reshape(variables, 1, width)

    @pl.when(has_after)
    def _():
        out_ref[:, row_count - 1 :, :] += recv_ref[after, pl.ds(halo_at, variables), :].reshape(
            variables, 1, width
        )


def local(
    adjoint,
    jac_diag,
    jac_face,
    metric,
    node_id,
    fringe_cell,
    donor_cell,
    fringe_weight,
    donor_count,
):
    adj, diag, face, met = adjoint[0], jac_diag[0], jac_face[0], metric[0]
    variables, row_count, width = adj.shape
    faces = face.shape[1]
    coords, corners = met.shape[1:3]
    doms, grids = lax.axis_size("dom"), lax.axis_size("grid")
    peers = doms * grids
    node_rows = coords * NODE_DEV // width
    used = node_rows + 2 * variables
    sent_rows = ceil_to(used, 8)
    spans = peers * NODE_DEV // SPAN
    params = pltpu.CompilerParams(vmem_limit_bytes=VMEM_BYTES)

    rows = 16 if spans <= 64 else 8
    steps = row_count // rows
    share = peers // steps
    edge = 8
    sent = pl.pallas_call(
        gather_and_nodes,
        grid=(steps,),
        in_specs=[
            pl.BlockSpec((variables, row_count, width), lambda s: (0, 0, 0)),
            pl.BlockSpec((variables, coords, corners, rows, width), lambda s: (0, 0, 0, s, 0)),
            pl.BlockSpec((corners, rows, width), lambda s: (0, s, 0)),
            pl.BlockSpec((pl.Squeezed(), share, width), lambda s: (s, 0, 0)),
            pl.BlockSpec((variables, 1, variables, edge, width), lambda s: (0, 0, 0, 0, 0)),
            pl.BlockSpec((variables, 1, variables, edge, width), lambda s: (0, 1, 0, row_count // edge - 1, 0)),
        ],
        out_specs=pl.BlockSpec((peers, sent_rows, width), lambda s: (0, 0, 0)),
        scratch_shapes=[
            pltpu.VMEM((2 * coords * spans, SPAN), jnp.float32),
            pltpu.VMEM((variables * row_count, 2 * width), jnp.bfloat16),
        ],
        out_shape=jax.ShapeDtypeStruct((peers, sent_rows, width), jnp.float32),
        compiler_params=pltpu.CompilerParams(vmem_limit_bytes=62 * 1024 * 1024),
        cost_estimate=pl.CostEstimate(
            flops=4 * coords * spans * SPAN * corners * row_count * width,
            bytes_accessed=met.size * 4,
            transcendentals=0,
        ),
        name="gather_and_nodes",
    )(adj, met, node_id[0], fringe_cell[0].reshape(steps, share, width), face, face)

    received = lax.all_to_all(sent, ("dom", "grid"), split_axis=0, concat_axis=0, tiled=True)

    vmem = pl.BlockSpec(memory_space=pltpu.VMEM)
    base, minus_weight = pl.pallas_call(
        jacobian,
        grid=(variables,),
        in_specs=[
            pl.BlockSpec(memory_space=pltpu.SMEM),
            pl.BlockSpec((peers, width), lambda j: (0, 0)),
            pl.BlockSpec((variables, row_count, width), lambda j: (0, 0, 0)),
            pl.BlockSpec((variables, pl.Squeezed(), row_count, width), lambda j: (0, j, 0, 0)),
            pl.BlockSpec((variables, faces, pl.Squeezed(), row_count, width), lambda j: (0, 0, j, 0, 0)),
        ],
        out_specs=[
            pl.BlockSpec((pl.Squeezed(), row_count, width), lambda j: (j, 0, 0)),
            pl.BlockSpec((peers, width), lambda j: (0, 0)),
        ],
        out_shape=[
            jax.ShapeDtypeStruct((variables, row_count, width), jnp.float32),
            jax.ShapeDtypeStruct((peers, width), jnp.float32),
        ],
        compiler_params=pltpu.CompilerParams(vmem_limit_bytes=40 * 1024 * 1024),
        cost_estimate=pl.CostEstimate(
            flops=2 * (diag.size + face.size), bytes_accessed=4 * (diag.size + face.size), transcendentals=0
        ),
        name="jacobian",
    )(donor_count, fringe_weight[0], adj, diag, face)

    product, node_sens = pl.pallas_call(
        finish,
        in_specs=[vmem] * 4,
        out_specs=[vmem] * 2,
        out_shape=[
            jax.ShapeDtypeStruct((variables, row_count, width), jnp.float32),
            jax.ShapeDtypeStruct((coords, NODE_DEV), jnp.float32),
        ],
        compiler_params=pltpu.CompilerParams(vmem_limit_bytes=20 * 1024 * 1024),
        name="finish",
    )(received, donor_cell[0], minus_weight, base)
    return (product[None], node_sens)


def solution(mesh):
    in_specs = (
        P("grid", None, "dom", None),
        P("grid", None, None, "dom", None),
        P("grid", None, None, None, "dom", None),
        P("grid", None, None, None, "dom", None),
        P("grid", None, "dom", None),
        P(("dom", "grid"), None, None),
        P(("dom", "grid"), None, None),
        P(("dom", "grid"), None, None),
        P(("dom", "grid"), None),
    )
    out_specs = (P("grid", None, "dom", None), P(None, ("dom", "grid")))
    return jax.shard_map(local, mesh=mesh, in_specs=in_specs, out_specs=out_specs, check_vma=False)
```

```python
import functools

import jax
import jax.numpy as jnp
from jax import lax
from jax.experimental import pallas as pl
from jax.experimental.pallas import tpu as pltpu
from jax.sharding import PartitionSpec as P

NODE_DEV = 512
LANES = 128
SPAN = 256
SPAN_BITS = SPAN.bit_length() - 1
CHUNK = 32
GROUP = 16
PAIR = 2
ROWS = 32
VMEM_BYTES = 62 * 1024 * 1024
LAST_WITH_LAST = (((1,), (1,)), ((), ()))


def shifted(block, axis, distance):
    devices = range(lax.axis_size(axis))
    route = [(i - distance, i) for i in devices if i - distance in devices]
    return lax.ppermute(block, axis, route)


def sublane_iota(count):
    return lax.broadcasted_iota(jnp.int32, (count, LANES), 0).astype(jnp.bfloat16)


def as_code(index):
    return index.astype(jnp.float32).astype(jnp.bfloat16)


def two_parts(value):
    head = value.astype(jnp.bfloat16)
    tail = (value - head.astype(jnp.float32)).astype(jnp.bfloat16)
    return head, tail


def weighted_sum(load, adj):
    running = load(0) * adj[0]
    for variable in range(1, len(adj)):
        running = running + load(variable) * adj[variable]
    return running


def cells_and_nodes(
    adj_ref,
    fringe_ref,
    node_ref,
    metric_hbm,
    diag_hbm,
    face_hbm,
    sent_ref,
    down_ref,
    up_ref,
    base_ref,
    totals,
    split_adj,
    metric_part,
    diag_part,
    face_part,
    edge_down,
    edge_up,
    metric_sem,
    diag_sem,
    face_sem,
):
    variables, row_count, width = adj_ref.shape
    steps, _, coords, corners, rows = metric_part.shape[:5]
    peers = sent_ref.shape[0]
    spans = totals.shape[0] // (2 * coords)
    span_rows = SPAN // width
    cell_spans = row_count // span_rows
    payload_at = coords * NODE_DEV // width
    zero = jnp.zeros((), jnp.bfloat16)
    one = jnp.ones((), jnp.bfloat16)

    def copies(step):
        at = pl.ds(pl.multiple_of(step * rows, rows), rows)
        return (
            pltpu.make_async_copy(metric_hbm.at[:, :, :, at, :], metric_part.at[step], metric_sem.at[step]),
            pltpu.make_async_copy(diag_hbm.at[:, :, at, :], diag_part.at[step], diag_sem.at[step]),
            pltpu.make_async_copy(face_hbm.at[:, :, :, at, :], face_part.at[step], face_sem.at[step]),
        )

    for step in range(steps):
        for copy in copies(step):
            copy.start()

    for i in range(variables):
        for half in range(span_rows):
            for part, piece in enumerate(two_parts(adj_ref[i, pl.ds(half, cell_spans, stride=span_rows), :])):
                at = part * SPAN + half * width
                split_adj[pl.ds(i * cell_spans, cell_spans), pl.ds(at, width)] = piece
    totals[...] = jnp.zeros_like(totals)

    place_code = sublane_iota(SPAN)
    cell_rows = lax.broadcasted_iota(jnp.int32, (cell_spans, width), 0)
    group = min(GROUP, peers)

    def gather(turn, none):
        picks = []
        for k in range(group):
            inside = fringe_ref[pl.ds(turn * group + k, 1), :] & (SPAN - 1)
            pick = jnp.where(place_code == as_code(inside), one, zero)
            picks.append(jnp.concatenate([pick, pick], axis=0))
        found = jnp.dot(split_adj[...], jnp.concatenate(picks, axis=1), preferred_element_type=jnp.float32)
        for k in range(group):
            q = turn * group + k
            mine = cell_rows == fringe_ref[pl.ds(q, 1), :] >> SPAN_BITS
            for i in range(variables):
                part = found[i * cell_spans : (i + 1) * cell_spans, k * width : (k + 1) * width]
                line = jnp.sum(jnp.where(mine, part, 0.0), axis=0, keepdims=True)
                at = payload_at + i
                sent_ref[q, at // PAIR, pl.ds(at % PAIR, 1), :] = line
        return none

    lax.fori_loop(0, peers // group, gather, 0)

    span_code = sublane_iota(spans)
    row_ids = lax.broadcasted_iota(jnp.int32, (rows, width), 0)
    lane_ids = lax.broadcasted_iota(jnp.int32, (rows, width), 1)

    def cells(step, none):
        for copy in copies(step):
            copy.wait()
        here = pl.ds(pl.multiple_of(step * rows, rows), rows)
        adj = [adj_ref[i, here, :] for i in range(variables)]
        for j in range(variables):
            total = weighted_sum(lambda i: diag_part[step, i, j], adj)
            faces = [weighted_sum(lambda i: face_part[step, i, f, j], adj) for f in range(4)]
            below = pltpu.roll(faces[0], rows - 1, 0)
            total = total + jnp.where(row_ids < rows - 1, below, 0.0)
            above = pltpu.roll(faces[1], 1, 0)
            total = total + jnp.where(row_ids > 0, above, 0.0)
            right = pltpu.roll(faces[2], width - 1, 1)
            total = total + jnp.where(lane_ids < width - 1, right, 0.0)
            left = pltpu.roll(faces[3], 1, 1)
            base_ref[j, here, :] = total + jnp.where(lane_ids > 0, left, 0.0)
            edge_down[step, pl.ds(j, 1), :] = faces[0][:1]
            edge_up[step, pl.ds(j, 1), :] = faces[1][rows - 1 :]

        left = []
        right = []
        for corner in range(corners):
            ids = node_ref[corner, here, :]
            span = ids >> SPAN_BITS
            owner_rows = NODE_DEV // SPAN
            span = (span & (owner_rows - 1)) * peers + (span >> (owner_rows.bit_length() - 1))
            span = as_code(span)
            inside = as_code(ids & (SPAN - 1))
            values = []
            for x in range(coords):
                values.extend(two_parts(weighted_sum(lambda i: metric_part[step, i, x, corner], adj)))
            for r in range(rows):
                hit = span_code == span[r : r + 1]
                left.append(jnp.concatenate([jnp.where(hit, v[r : r + 1], zero) for v in values], axis=0))
                right.append(jnp.where(place_code == inside[r : r + 1], one, zero))
        added = lax.dot_general(
            jnp.concatenate(left, axis=1),
            jnp.concatenate(right, axis=1),
            LAST_WITH_LAST,
            preferred_element_type=jnp.float32,
        )
        totals[...] = totals[...] + added
        return none

    lax.fori_loop(0, steps, cells, 0)

    for step in range(1, steps):
        for j in range(variables):
            base_ref[j, pl.ds(step * rows - 1, 1), :] += edge_down[step, pl.ds(j, 1), :]
            base_ref[j, pl.ds(step * rows, 1), :] += edge_up[step - 1, pl.ds(j, 1), :]
    down_ref[...] = edge_down[0, :variables, :]
    up_ref[...] = edge_up[steps - 1, :variables, :]

    for x in range(coords):
        both = totals[pl.ds(2 * x * spans, spans), :] + totals[pl.ds((2 * x + 1) * spans, spans), :]
        for part in range(NODE_DEV // SPAN):
            for half in range(span_rows):
                at = (x * (NODE_DEV // SPAN) + part) * span_rows + half
                sent_ref[:, at // PAIR, at % PAIR, :] = both[
                    part * peers : (part + 1) * peers, half * width : (half + 1) * width
                ]


def prepare(count_ref, weight_ref, base_ref, minus_ref, out_ref):
    peers, width = weight_ref.shape
    slot = lax.broadcasted_iota(jnp.int32, (1, width), 1)
    for q in range(peers):
        minus_ref[pl.ds(q, 1), :] = jnp.where(slot < count_ref[0, q], -weight_ref[pl.ds(q, 1), :], 0.0)
    out_ref[...] = base_ref[...]


def finish(recv_ref, down_ref, up_ref, cell_ref, weight_ref, base_ref, out_ref, sens_ref):
    variables, row_count, width = base_ref.shape
    peers = recv_ref.shape[0]
    coords = sens_ref.shape[0]
    node_rows = coords * NODE_DEV // width
    payload_at = node_rows
    spans = row_count * width // SPAN
    span_rows = SPAN // width
    zero = jnp.zeros((), jnp.bfloat16)
    one = jnp.ones((), jnp.bfloat16)

    sums = [jnp.sum(recv_ref[:, at, :, :], axis=0) for at in range(node_rows // PAIR)]
    per_coord = node_rows // coords
    for x in range(coords):
        for part in range(per_coord):
            at = x * per_coord + part
            sens_ref[pl.ds(x, 1), pl.ds(part * width, width)] = sums[at // PAIR][at % PAIR : at % PAIR + 1]

    span_code = sublane_iota(spans)
    place_code = sublane_iota(SPAN)
    payload = []
    for i in range(variables):
        at = payload_at + i
        payload.append(two_parts(recv_ref[:, at // PAIR, at % PAIR, :] * weight_ref[...]))
    chunk = min(CHUNK, peers)
    for start in range(0, peers, chunk):
        left = []
        right = []
        for q in range(start, start + chunk):
            cell = cell_ref[pl.ds(q, 1), :]
            hit = span_code == as_code(cell >> SPAN_BITS)
            left.append(
                jnp.concatenate(
                    [jnp.where(hit, v[q : q + 1], zero) for values in payload for v in values], axis=0
                )
            )
            right.append(jnp.where(place_code == as_code(cell & (SPAN - 1)), one, zero))
        added = lax.dot_general(
            jnp.concatenate(left, axis=1),
            jnp.concatenate(right, axis=1),
            LAST_WITH_LAST,
            preferred_element_type=jnp.float32,
        )
        source = base_ref if start == 0 else out_ref
        for i in range(variables):
            both = added[2 * i * spans : (2 * i + 1) * spans] + added[(2 * i + 1) * spans : (2 * i + 2) * spans]
            for half in range(span_rows):
                where = pl.ds(half, spans, stride=span_rows)
                out_ref[i, where, :] = source[i, where, :] + both[:, half * width : (half + 1) * width]

    for i in range(variables):
        out_ref[i, pl.ds(row_count - 1, 1), :] += down_ref[pl.ds(i, 1), :]
        out_ref[i, pl.ds(0, 1), :] += up_ref[pl.ds(i, 1), :]


def local(
    adjoint,
    jac_diag,
    jac_face,
    metric,
    node_id,
    fringe_cell,
    donor_cell,
    fringe_weight,
    donor_count,
):
    adj, diag, face, met = adjoint[0], jac_diag[0], jac_face[0], metric[0]
    variables, row_count, width = adj.shape
    faces = face.shape[1]
    coords, corners = met.shape[1:3]
    doms, grids = lax.axis_size("dom"), lax.axis_size("grid")
    peers = doms * grids
    node_rows = coords * NODE_DEV // width
    sent_shape = (peers, (node_rows + variables) // PAIR, PAIR, width)
    spans = peers * NODE_DEV // SPAN
    params = pltpu.CompilerParams(vmem_limit_bytes=VMEM_BYTES)

    rows = ROWS if spans <= 64 else 8
    steps = row_count // rows
    vmem = pl.BlockSpec(memory_space=pltpu.VMEM)
    smem = pl.BlockSpec(memory_space=pltpu.SMEM)
    hbm = pl.BlockSpec(memory_space=pl.ANY)
    sent, down, up, base = pl.pallas_call(
        cells_and_nodes,
        in_specs=[vmem] * 3 + [hbm] * 3,
        out_specs=[vmem] * 4,
        out_shape=[
            jax.ShapeDtypeStruct(sent_shape, jnp.float32),
            jax.ShapeDtypeStruct((variables, width), jnp.float32),
            jax.ShapeDtypeStruct((variables, width), jnp.float32),
            jax.ShapeDtypeStruct((variables, row_count, width), jnp.float32),
        ],
        scratch_shapes=[
            pltpu.VMEM((2 * coords * spans, SPAN), jnp.float32),
            pltpu.VMEM((variables * row_count * width // SPAN, 2 * SPAN), jnp.bfloat16),
            pltpu.VMEM((steps, variables, coords, corners, rows, width), jnp.float32),
            pltpu.VMEM((steps, variables, variables, rows, width), jnp.float32),
            pltpu.VMEM((steps, variables, faces, variables, rows, width), jnp.float32),
            pltpu.VMEM((steps, 8, width), jnp.float32),
            pltpu.VMEM((steps, 8, width), jnp.float32),
            pltpu.SemaphoreType.DMA((steps,)),
            pltpu.SemaphoreType.DMA((steps,)),
            pltpu.SemaphoreType.DMA((steps,)),
        ],
        compiler_params=pltpu.CompilerParams(vmem_limit_bytes=VMEM_BYTES),
        cost_estimate=pl.CostEstimate(
            flops=4 * coords * spans * SPAN * corners * row_count * width,
            bytes_accessed=4 * (met.size + diag.size + face.size),
            transcendentals=0,
        ),
        name="cells_and_nodes",
    )(adj, fringe_cell[0], node_id[0], met, diag, face)

    received = lax.all_to_all(sent, ("dom", "grid"), split_axis=0, concat_axis=0, tiled=True)
    from_below = shifted(down, "dom", -1)
    from_above = shifted(up, "dom", 1)

    minus_weight, held = pl.pallas_call(
        prepare,
        in_specs=[smem] + [vmem] * 2,
        out_specs=[vmem] * 2,
        out_shape=[
            jax.ShapeDtypeStruct((peers, width), jnp.float32),
            jax.ShapeDtypeStruct((variables, row_count, width), jnp.float32),
        ],
        compiler_params=pltpu.CompilerParams(vmem_limit_bytes=20 * 1024 * 1024),
        cost_estimate=pl.CostEstimate(flops=base.size, bytes_accessed=8 * base.size, transcendentals=0),
        name="prepare",
    )(donor_count, fringe_weight[0], base)

    product, node_sens = pl.pallas_call(
        finish,
        in_specs=[vmem] * 6,
        out_specs=[vmem] * 2,
        out_shape=[
            jax.ShapeDtypeStruct((variables, row_count, width), jnp.float32),
            jax.ShapeDtypeStruct((coords, NODE_DEV), jnp.float32),
        ],
        compiler_params=pltpu.CompilerParams(vmem_limit_bytes=20 * 1024 * 1024),
        name="finish",
    )(received, from_below, from_above, donor_cell[0], minus_weight, held)
    return (product[None], node_sens)


def solution(mesh):
    in_specs = (
        P("grid", None, "dom", None),
        P("grid", None, None, "dom", None),
        P("grid", None, None, None, "dom", None),
        P("grid", None, None, None, "dom", None),
        P("grid", None, "dom", None),
        P(("dom", "grid"), None, None),
        P(("dom", "grid"), None, None),
        P(("dom", "grid"), None, None),
        P(("dom", "grid"), None),
    )
    out_specs = (P("grid", None, "dom", None), P(None, ("dom", "grid")))
    return jax.shard_map(local, mesh=mesh, in_specs=in_specs, out_specs=out_specs, check_vma=False)
```

```python
import functools

import jax
import jax.numpy as jnp
from jax import lax
from jax.experimental import pallas as pl
from jax.experimental.pallas import tpu as pltpu
from jax.sharding import PartitionSpec as P

NODE_DEV = 512
LANES = 128
SPAN = 256
SPAN_BITS = SPAN.bit_length() - 1
CHUNK = 32
GROUP = 32
PAIR = 2
ROWS = 32
VMEM_BYTES = 62 * 1024 * 1024
LAST_WITH_LAST = (((1,), (1,)), ((), ()))


def shifted(block, axis, distance):
    devices = range(lax.axis_size(axis))
    route = [(i - distance, i) for i in devices if i - distance in devices]
    return lax.ppermute(block, axis, route)


def sublane_iota(count):
    return lax.broadcasted_iota(jnp.int32, (count, LANES), 0).astype(jnp.bfloat16)


def as_code(index):
    return index.astype(jnp.float32).astype(jnp.bfloat16)


def two_parts(value):
    head = value.astype(jnp.bfloat16)
    tail = (value - head.astype(jnp.float32)).astype(jnp.bfloat16)
    return head, tail


def weighted_sum(load, adj):
    running = load(0) * adj[0]
    for variable in range(1, len(adj)):
        running = running + load(variable) * adj[variable]
    return running


def cells_and_nodes(
    adj_ref,
    fringe_ref,
    node_ref,
    metric_hbm,
    diag_hbm,
    face_hbm,
    sent_ref,
    down_ref,
    up_ref,
    base_ref,
    edge_down,
    edge_up,
    totals,
    split_adj,
    metric_part,
    diag_part,
    face_part,
    metric_sem,
    diag_sem,
    face_sem,
):
    variables, row_count, width = adj_ref.shape
    steps, _, coords, corners, rows = metric_part.shape[:5]
    peers = sent_ref.shape[0]
    spans = totals.shape[0] // (2 * coords)
    span_rows = SPAN // width
    cell_spans = row_count // span_rows
    payload_at = coords * NODE_DEV // width
    zero = jnp.zeros((), jnp.bfloat16)
    one = jnp.ones((), jnp.bfloat16)

    def copies(step):
        at = pl.ds(pl.multiple_of(step * rows, rows), rows)
        return (
            pltpu.make_async_copy(metric_hbm.at[:, :, :, at, :], metric_part.at[step], metric_sem.at[step]),
            pltpu.make_async_copy(diag_hbm.at[:, :, at, :], diag_part.at[step], diag_sem.at[step]),
            pltpu.make_async_copy(face_hbm.at[:, :, :, at, :], face_part.at[step], face_sem.at[step]),
        )

    for step in range(steps):
        for copy in copies(step):
            copy.start()

    for i in range(variables):
        for half in range(span_rows):
            for part, piece in enumerate(two_parts(adj_ref[i, pl.ds(half, cell_spans, stride=span_rows), :])):
                at = part * SPAN + half * width
                split_adj[pl.ds(i * cell_spans, cell_spans), pl.ds(at, width)] = piece
    totals[...] = jnp.zeros_like(totals)

    place_code = sublane_iota(SPAN)
    cell_rows = lax.broadcasted_iota(jnp.int32, (cell_spans, width), 0)
    group = min(GROUP, peers)

    def gather(turn, none):
        picks = []
        for k in range(group):
            inside = fringe_ref[pl.ds(turn * group + k, 1), :] & (SPAN - 1)
            pick = jnp.where(place_code == as_code(inside), one, zero)
            picks.append(jnp.concatenate([pick, pick], axis=0))
        found = jnp.dot(split_adj[...], jnp.concatenate(picks, axis=1), preferred_element_type=jnp.float32)
        for k in range(group):
            q = turn * group + k
            mine = cell_rows == fringe_ref[pl.ds(q, 1), :] >> SPAN_BITS
            for i in range(variables):
                part = found[i * cell_spans : (i + 1) * cell_spans, k * width : (k + 1) * width]
                line = jnp.sum(jnp.where(mine, part, 0.0), axis=0, keepdims=True)
                at = payload_at + i
                sent_ref[q, at // PAIR, pl.ds(at % PAIR, 1), :] = line
        return none

    lax.fori_loop(0, peers // group, gather, 0)

    span_code = sublane_iota(spans)
    row_ids = lax.broadcasted_iota(jnp.int32, (rows, width), 0)
    lane_ids = lax.broadcasted_iota(jnp.int32, (rows, width), 1)

    def cells(step, none):
        for copy in copies(step):
            copy.wait()
        here = pl.ds(pl.multiple_of(step * rows, rows), rows)
        adj = [adj_ref[i, here, :] for i in range(variables)]
        for j in range(variables):
            total = weighted_sum(lambda i: diag_part[step, i, j], adj)
            faces = [weighted_sum(lambda i: face_part[step, i, f, j], adj) for f in range(4)]
            below = pltpu.roll(faces[0], rows - 1, 0)
            total = total + jnp.where(row_ids < rows - 1, below, 0.0)
            above = pltpu.roll(faces[1], 1, 0)
            total = total + jnp.where(row_ids > 0, above, 0.0)
            right = pltpu.roll(faces[2], width - 1, 1)
            total = total + jnp.where(lane_ids < width - 1, right, 0.0)
            left = pltpu.roll(faces[3], 1, 1)
            base_ref[j, here, :] = total + jnp.where(lane_ids > 0, left, 0.0)
            edge_down[step, pl.ds(j, 1), :] = faces[0][:1]
            edge_up[step, pl.ds(j, 1), :] = faces[1][rows - 1 :]

        left = []
        right = []
        for corner in range(corners):
            ids = node_ref[corner, here, :]
            span = ids >> SPAN_BITS
            owner_rows = NODE_DEV // SPAN
            span = (span & (owner_rows - 1)) * peers + (span >> (owner_rows.bit_length() - 1))
            span = as_code(span)
            inside = as_code(ids & (SPAN - 1))
            values = []
            for x in range(coords):
                values.extend(two_parts(weighted_sum(lambda i: metric_part[step, i, x, corner], adj)))
            for r in range(rows):
                hit = span_code == span[r : r + 1]
                left.append(jnp.concatenate([jnp.where(hit, v[r : r + 1], zero) for v in values], axis=0))
                right.append(jnp.where(place_code == inside[r : r + 1], one, zero))
        added = lax.dot_general(
            jnp.concatenate(left, axis=1),
            jnp.concatenate(right, axis=1),
            LAST_WITH_LAST,
            preferred_element_type=jnp.float32,
        )
        totals[...] = totals[...] + added
        return none

    lax.fori_loop(0, steps, cells, 0)

    down_ref[...] = edge_down[0, :variables, :]
    up_ref[...] = edge_up[steps - 1, :variables, :]

    for x in range(coords):
        both = totals[pl.ds(2 * x * spans, spans), :] + totals[pl.ds((2 * x + 1) * spans, spans), :]
        for part in range(NODE_DEV // SPAN):
            for half in range(span_rows):
                at = (x * (NODE_DEV // SPAN) + part) * span_rows + half
                sent_ref[:, at // PAIR, at % PAIR, :] = both[
                    part * peers : (part + 1) * peers, half * width : (half + 1) * width
                ]


def prepare(count_ref, weight_ref, base_ref, edge_down, edge_up, minus_ref, out_ref):
    variables, row_count = base_ref.shape[:2]
    steps = edge_down.shape[0]
    rows = row_count // steps
    peers, width = weight_ref.shape
    slot = lax.broadcasted_iota(jnp.int32, (1, width), 1)
    for q in range(peers):
        minus_ref[pl.ds(q, 1), :] = jnp.where(slot < count_ref[0, q], -weight_ref[pl.ds(q, 1), :], 0.0)
    out_ref[...] = base_ref[...]
    for step in range(1, steps):
        for j in range(variables):
            out_ref[j, pl.ds(step * rows - 1, 1), :] += edge_down[step, pl.ds(j, 1), :]
            out_ref[j, pl.ds(step * rows, 1), :] += edge_up[step - 1, pl.ds(j, 1), :]


def finish(recv_ref, down_ref, up_ref, cell_ref, weight_ref, base_ref, out_ref, sens_ref):
    variables, row_count, width = base_ref.shape
    peers = recv_ref.shape[0]
    coords = sens_ref.shape[0]
    node_rows = coords * NODE_DEV // width
    payload_at = node_rows
    spans = row_count * width // SPAN
    span_rows = SPAN // width
    zero = jnp.zeros((), jnp.bfloat16)
    one = jnp.ones((), jnp.bfloat16)

    sums = [jnp.sum(recv_ref[:, at, :, :], axis=0) for at in range(node_rows // PAIR)]
    per_coord = node_rows // coords
    for x in range(coords):
        for part in range(per_coord):
            at = x * per_coord + part
            sens_ref[pl.ds(x, 1), pl.ds(part * width, width)] = sums[at // PAIR][at % PAIR : at % PAIR + 1]

    span_code = sublane_iota(spans)
    place_code = sublane_iota(SPAN)
    payload = []
    for i in range(variables):
        at = payload_at + i
        payload.append(two_parts(recv_ref[:, at // PAIR, at % PAIR, :] * weight_ref[...]))
    chunk = min(CHUNK, peers)
    for start in range(0, peers, chunk):
        left = []
        right = []
        for q in range(start, start + chunk):
            cell = cell_ref[pl.ds(q, 1), :]
            hit = span_code == as_code(cell >> SPAN_BITS)
            left.append(
                jnp.concatenate(
                    [jnp.where(hit, v[q : q + 1], zero) for values in payload for v in values], axis=0
                )
            )
            right.append(jnp.where(place_code == as_code(cell & (SPAN - 1)), one, zero))
        added = lax.dot_general(
            jnp.concatenate(left, axis=1),
            jnp.concatenate(right, axis=1),
            LAST_WITH_LAST,
            preferred_element_type=jnp.float32,
        )
        source = base_ref if start == 0 else out_ref
        for i in range(variables):
            both = added[2 * i * spans : (2 * i + 1) * spans] + added[(2 * i + 1) * spans : (2 * i + 2) * spans]
            for half in range(span_rows):
                where = pl.ds(half, spans, stride=span_rows)
                out_ref[i, where, :] = source[i, where, :] + both[:, half * width : (half + 1) * width]

    for i in range(variables):
        out_ref[i, pl.ds(row_count - 1, 1), :] += down_ref[pl.ds(i, 1), :]
        out_ref[i, pl.ds(0, 1), :] += up_ref[pl.ds(i, 1), :]


def local(
    adjoint,
    jac_diag,
    jac_face,
    metric,
    node_id,
    fringe_cell,
    donor_cell,
    fringe_weight,
    donor_count,
):
    adj, diag, face, met = adjoint[0], jac_diag[0], jac_face[0], metric[0]
    variables, row_count, width = adj.shape
    faces = face.shape[1]
    coords, corners = met.shape[1:3]
    doms, grids = lax.axis_size("dom"), lax.axis_size("grid")
    peers = doms * grids
    node_rows = coords * NODE_DEV // width
    sent_shape = (peers, (node_rows + variables) // PAIR, PAIR, width)
    spans = peers * NODE_DEV // SPAN
    params = pltpu.CompilerParams(vmem_limit_bytes=VMEM_BYTES)

    rows = ROWS if spans <= 64 else 8
    steps = row_count // rows
    vmem = pl.BlockSpec(memory_space=pltpu.VMEM)
    smem = pl.BlockSpec(memory_space=pltpu.SMEM)
    hbm = pl.BlockSpec(memory_space=pl.ANY)
    sent, down, up, base, edge_down, edge_up = pl.pallas_call(
        cells_and_nodes,
        in_specs=[vmem] * 3 + [hbm] * 3,
        out_specs=[vmem] * 6,
        out_shape=[
            jax.ShapeDtypeStruct(sent_shape, jnp.float32),
            jax.ShapeDtypeStruct((variables, width), jnp.float32),
            jax.ShapeDtypeStruct((variables, width), jnp.float32),
            jax.ShapeDtypeStruct((variables, row_count, width), jnp.float32),
            jax.ShapeDtypeStruct((steps, 8, width), jnp.float32),
            jax.ShapeDtypeStruct((steps, 8, width), jnp.float32),
        ],
        scratch_shapes=[
            pltpu.VMEM((2 * coords * spans, SPAN), jnp.float32),
            pltpu.VMEM((variables * row_count * width // SPAN, 2 * SPAN), jnp.bfloat16),
            pltpu.VMEM((steps, variables, coords, corners, rows, width), jnp.float32),
            pltpu.VMEM((steps, variables, variables, rows, width), jnp.float32),
            pltpu.VMEM((steps, variables, faces, variables, rows, width), jnp.float32),
            pltpu.SemaphoreType.DMA((steps,)),
            pltpu.SemaphoreType.DMA((steps,)),
            pltpu.SemaphoreType.DMA((steps,)),
        ],
        compiler_params=pltpu.CompilerParams(vmem_limit_bytes=VMEM_BYTES),
        cost_estimate=pl.CostEstimate(
            flops=4 * coords * spans * SPAN * corners * row_count * width,
            bytes_accessed=4 * (met.size + diag.size + face.size),
            transcendentals=0,
        ),
        name="cells_and_nodes",
    )(adj, fringe_cell[0], node_id[0], met, diag, face)

    received = lax.all_to_all(sent, ("dom", "grid"), split_axis=0, concat_axis=0, tiled=True)
    from_below = shifted(down, "dom", -1)
    from_above = shifted(up, "dom", 1)

    minus_weight, held = pl.pallas_call(
        prepare,
        in_specs=[smem] + [vmem] * 4,
        out_specs=[vmem] * 2,
        out_shape=[
            jax.ShapeDtypeStruct((peers, width), jnp.float32),
            jax.ShapeDtypeStruct((variables, row_count, width), jnp.float32),
        ],
        compiler_params=pltpu.CompilerParams(vmem_limit_bytes=20 * 1024 * 1024),
        cost_estimate=pl.CostEstimate(flops=base.size, bytes_accessed=8 * base.size, transcendentals=0),
        name="prepare",
    )(donor_count, fringe_weight[0], base, edge_down, edge_up)

    product, node_sens = pl.pallas_call(
        finish,
        in_specs=[vmem] * 6,
        out_specs=[vmem] * 2,
        out_shape=[
            jax.ShapeDtypeStruct((variables, row_count, width), jnp.float32),
            jax.ShapeDtypeStruct((coords, NODE_DEV), jnp.float32),
        ],
        compiler_params=pltpu.CompilerParams(vmem_limit_bytes=20 * 1024 * 1024),
        name="finish",
    )(received, from_below, from_above, donor_cell[0], minus_weight, held)
    return (product[None], node_sens)


def solution(mesh):
    in_specs = (
        P("grid", None, "dom", None),
        P("grid", None, None, "dom", None),
        P("grid", None, None, None, "dom", None),
        P("grid", None, None, None, "dom", None),
        P("grid", None, "dom", None),
        P(("dom", "grid"), None, None),
        P(("dom", "grid"), None, None),
        P(("dom", "grid"), None, None),
        P(("dom", "grid"), None),
    )
    out_specs = (P("grid", None, "dom", None), P(None, ("dom", "grid")))
    return jax.shard_map(local, mesh=mesh, in_specs=in_specs, out_specs=out_specs, check_vma=False)
```

```python
import functools

import jax
import jax.numpy as jnp
from jax import lax
from jax.experimental import pallas as pl
from jax.experimental.pallas import tpu as pltpu
from jax.sharding import PartitionSpec as P

NODE_DEV = 512
LANES = 128
SPAN = 256
SPAN_BITS = SPAN.bit_length() - 1
CHUNK = 32
GROUP = 16
PAIR = 2
ROWS = 32
VMEM_BYTES = 62 * 1024 * 1024
LAST_WITH_LAST = (((1,), (1,)), ((), ()))


def shifted(block, axis, distance):
    devices = range(lax.axis_size(axis))
    route = [(i - distance, i) for i in devices if i - distance in devices]
    return lax.ppermute(block, axis, route)


def sublane_iota(count):
    return lax.broadcasted_iota(jnp.int32, (count, LANES), 0).astype(jnp.bfloat16)


def as_code(index):
    return index.astype(jnp.float32).astype(jnp.bfloat16)


def two_parts(value):
    head = value.astype(jnp.bfloat16)
    tail = (value - head.astype(jnp.float32)).astype(jnp.bfloat16)
    return head, tail


def weighted_sum(load, adj):
    running = load(0) * adj[0]
    for variable in range(1, len(adj)):
        running = running + load(variable) * adj[variable]
    return running


def cells_and_nodes(
    adj_ref,
    fringe_ref,
    node_ref,
    metric_hbm,
    diag_hbm,
    face_hbm,
    sent_ref,
    down_ref,
    up_ref,
    base_ref,
    totals,
    split_adj,
    metric_part,
    diag_part,
    face_part,
    edge_down,
    edge_up,
    metric_sem,
    diag_sem,
    face_sem,
):
    variables, row_count, width = adj_ref.shape
    steps, _, coords, corners, rows = metric_part.shape[:5]
    peers = sent_ref.shape[0]
    spans = totals.shape[0] // (2 * coords)
    span_rows = SPAN // width
    cell_spans = row_count // span_rows
    payload_at = coords * NODE_DEV // width
    zero = jnp.zeros((), jnp.bfloat16)
    one = jnp.ones((), jnp.bfloat16)

    def copies(step):
        at = pl.ds(pl.multiple_of(step * rows, rows), rows)
        found = []
        for i in range(variables):
            found += [
                pltpu.make_async_copy(metric_hbm.at[i, :, :, at, :], metric_part.at[step, i], metric_sem.at[step, i]),
                pltpu.make_async_copy(diag_hbm.at[i, :, at, :], diag_part.at[step, i], diag_sem.at[step, i]),
                pltpu.make_async_copy(face_hbm.at[i, :, :, at, :], face_part.at[step, i], face_sem.at[step, i]),
            ]
        return found

    for copy in copies(0):
        copy.start()

    for i in range(variables):
        for half in range(span_rows):
            for part, piece in enumerate(two_parts(adj_ref[i, pl.ds(half, cell_spans, stride=span_rows), :])):
                at = part * SPAN + half * width
                split_adj[pl.ds(i * cell_spans, cell_spans), pl.ds(at, width)] = piece
    totals[...] = jnp.zeros_like(totals)

    place_code = sublane_iota(SPAN)
    cell_rows = lax.broadcasted_iota(jnp.int32, (cell_spans, width), 0)
    group = min(GROUP, peers)

    def gather(turn, none):
        picks = []
        for k in range(group):
            inside = fringe_ref[pl.ds(turn * group + k, 1), :] & (SPAN - 1)
            pick = jnp.where(place_code == as_code(inside), one, zero)
            picks.append(jnp.concatenate([pick, pick], axis=0))
        found = jnp.dot(split_adj[...], jnp.concatenate(picks, axis=1), preferred_element_type=jnp.float32)
        for k in range(group):
            q = turn * group + k
            mine = cell_rows == fringe_ref[pl.ds(q, 1), :] >> SPAN_BITS
            for i in range(variables):
                part = found[i * cell_spans : (i + 1) * cell_spans, k * width : (k + 1) * width]
                line = jnp.sum(jnp.where(mine, part, 0.0), axis=0, keepdims=True)
                at = payload_at + i
                sent_ref[q, at // PAIR, pl.ds(at % PAIR, 1), :] = line
        return none

    lax.fori_loop(0, peers // group, gather, 0)

    span_code = sublane_iota(spans)
    row_ids = lax.broadcasted_iota(jnp.int32, (rows, width), 0)
    lane_ids = lax.broadcasted_iota(jnp.int32, (rows, width), 1)

    def cells(step, none):
        @pl.when(step + 1 < steps)
        def _():
            for copy in copies(step + 1):
                copy.start()

        for copy in copies(step):
            copy.wait()
        here = pl.ds(pl.multiple_of(step * rows, rows), rows)
        adj = [adj_ref[i, here, :] for i in range(variables)]
        for j in range(variables):
            total = weighted_sum(lambda i: diag_part[step, i, j], adj)
            faces = [weighted_sum(lambda i: face_part[step, i, f, j], adj) for f in range(4)]
            below = pltpu.roll(faces[0], rows - 1, 0)
            total = total + jnp.where(row_ids < rows - 1, below, 0.0)
            above = pltpu.roll(faces[1], 1, 0)
            total = total + jnp.where(row_ids > 0, above, 0.0)
            right = pltpu.roll(faces[2], width - 1, 1)
            total = total + jnp.where(lane_ids < width - 1, right, 0.0)
            left = pltpu.roll(faces[3], 1, 1)
            base_ref[j, here, :] = total + jnp.where(lane_ids > 0, left, 0.0)
            edge_down[step, pl.ds(j, 1), :] = faces[0][:1]
            edge_up[step, pl.ds(j, 1), :] = faces[1][rows - 1 :]

        left = []
        right = []
        for corner in range(corners):
            ids = node_ref[corner, here, :]
            span = ids >> SPAN_BITS
            owner_rows = NODE_DEV // SPAN
            span = (span & (owner_rows - 1)) * peers + (span >> (owner_rows.bit_length() - 1))
            span = as_code(span)
            inside = as_code(ids & (SPAN - 1))
            values = []
            for x in range(coords):
                values.extend(two_parts(weighted_sum(lambda i: metric_part[step, i, x, corner], adj)))
            for r in range(rows):
                hit = span_code == span[r : r + 1]
                left.append(jnp.concatenate([jnp.where(hit, v[r : r + 1], zero) for v in values], axis=0))
                right.append(jnp.where(place_code == inside[r : r + 1], one, zero))
        added = lax.dot_general(
            jnp.concatenate(left, axis=1),
            jnp.concatenate(right, axis=1),
            LAST_WITH_LAST,
            preferred_element_type=jnp.float32,
        )
        totals[...] = totals[...] + added
        return none

    lax.fori_loop(0, steps, cells, 0)

    for step in range(1, steps):
        for j in range(variables):
            base_ref[j, pl.ds(step * rows - 1, 1), :] += edge_down[step, pl.ds(j, 1), :]
            base_ref[j, pl.ds(step * rows, 1), :] += edge_up[step - 1, pl.ds(j, 1), :]
    down_ref[...] = edge_down[0, :variables, :]
    up_ref[...] = edge_up[steps - 1, :variables, :]

    for x in range(coords):
        both = totals[pl.ds(2 * x * spans, spans), :] + totals[pl.ds((2 * x + 1) * spans, spans), :]
        for part in range(NODE_DEV // SPAN):
            for half in range(span_rows):
                at = (x * (NODE_DEV // SPAN) + part) * span_rows + half
                sent_ref[:, at // PAIR, at % PAIR, :] = both[
                    part * peers : (part + 1) * peers, half * width : (half + 1) * width
                ]


def prepare(count_ref, weight_ref, base_ref, minus_ref, out_ref):
    peers, width = weight_ref.shape
    slot = lax.broadcasted_iota(jnp.int32, (1, width), 1)
    for q in range(peers):
        minus_ref[pl.ds(q, 1), :] = jnp.where(slot < count_ref[0, q], -weight_ref[pl.ds(q, 1), :], 0.0)
    out_ref[...] = base_ref[...]


def finish(recv_ref, down_ref, up_ref, cell_ref, weight_ref, base_ref, out_ref, sens_ref):
    variables, row_count, width = base_ref.shape
    peers = recv_ref.shape[0]
    coords = sens_ref.shape[0]
    node_rows = coords * NODE_DEV // width
    payload_at = node_rows
    spans = row_count * width // SPAN
    span_rows = SPAN // width
    zero = jnp.zeros((), jnp.bfloat16)
    one = jnp.ones((), jnp.bfloat16)

    sums = [jnp.sum(recv_ref[:, at, :, :], axis=0) for at in range(node_rows // PAIR)]
    per_coord = node_rows // coords
    for x in range(coords):
        for part in range(per_coord):
            at = x * per_coord + part
            sens_ref[pl.ds(x, 1), pl.ds(part * width, width)] = sums[at // PAIR][at % PAIR : at % PAIR + 1]

    span_code = sublane_iota(spans)
    place_code = sublane_iota(SPAN)
    payload = []
    for i in range(variables):
        at = payload_at + i
        payload.append(two_parts(recv_ref[:, at // PAIR, at % PAIR, :] * weight_ref[...]))
    chunk = min(CHUNK, peers)
    for start in range(0, peers, chunk):
        left = []
        right = []
        for q in range(start, start + chunk):
            cell = cell_ref[pl.ds(q, 1), :]
            hit = span_code == as_code(cell >> SPAN_BITS)
            left.append(
                jnp.concatenate(
                    [jnp.where(hit, v[q : q + 1], zero) for values in payload for v in values], axis=0
                )
            )
            right.append(jnp.where(place_code == as_code(cell & (SPAN - 1)), one, zero))
        added = lax.dot_general(
            jnp.concatenate(left, axis=1),
            jnp.concatenate(right, axis=1),
            LAST_WITH_LAST,
            preferred_element_type=jnp.float32,
        )
        source = base_ref if start == 0 else out_ref
        for i in range(variables):
            both = added[2 * i * spans : (2 * i + 1) * spans] + added[(2 * i + 1) * spans : (2 * i + 2) * spans]
            for half in range(span_rows):
                where = pl.ds(half, spans, stride=span_rows)
                out_ref[i, where, :] = source[i, where, :] + both[:, half * width : (half + 1) * width]

    for i in range(variables):
        out_ref[i, pl.ds(row_count - 1, 1), :] += down_ref[pl.ds(i, 1), :]
        out_ref[i, pl.ds(0, 1), :] += up_ref[pl.ds(i, 1), :]


def local(
    adjoint,
    jac_diag,
    jac_face,
    metric,
    node_id,
    fringe_cell,
    donor_cell,
    fringe_weight,
    donor_count,
):
    adj, diag, face, met = adjoint[0], jac_diag[0], jac_face[0], metric[0]
    variables, row_count, width = adj.shape
    faces = face.shape[1]
    coords, corners = met.shape[1:3]
    doms, grids = lax.axis_size("dom"), lax.axis_size("grid")
    peers = doms * grids
    node_rows = coords * NODE_DEV // width
    sent_shape = (peers, (node_rows + variables) // PAIR, PAIR, width)
    spans = peers * NODE_DEV // SPAN
    params = pltpu.CompilerParams(vmem_limit_bytes=VMEM_BYTES)

    rows = ROWS if spans <= 64 else 8
    steps = row_count // rows
    vmem = pl.BlockSpec(memory_space=pltpu.VMEM)
    smem = pl.BlockSpec(memory_space=pltpu.SMEM)
    hbm = pl.BlockSpec(memory_space=pl.ANY)
    sent, down, up, base = pl.pallas_call(
        cells_and_nodes,
        in_specs=[vmem] * 3 + [hbm] * 3,
        out_specs=[vmem] * 4,
        out_shape=[
            jax.ShapeDtypeStruct(sent_shape, jnp.float32),
            jax.ShapeDtypeStruct((variables, width), jnp.float32),
            jax.ShapeDtypeStruct((variables, width), jnp.float32),
            jax.ShapeDtypeStruct((variables, row_count, width), jnp.float32),
        ],
        scratch_shapes=[
            pltpu.VMEM((2 * coords * spans, SPAN), jnp.float32),
            pltpu.VMEM((variables * row_count * width // SPAN, 2 * SPAN), jnp.bfloat16),
            pltpu.VMEM((steps, variables, coords, corners, rows, width), jnp.float32),
            pltpu.VMEM((steps, variables, variables, rows, width), jnp.float32),
            pltpu.VMEM((steps, variables, faces, variables, rows, width), jnp.float32),
            pltpu.VMEM((steps, 8, width), jnp.float32),
            pltpu.VMEM((steps, 8, width), jnp.float32),
            pltpu.SemaphoreType.DMA((steps, variables)),
            pltpu.SemaphoreType.DMA((steps, variables)),
            pltpu.SemaphoreType.DMA((steps, variables)),
        ],
        compiler_params=pltpu.CompilerParams(vmem_limit_bytes=VMEM_BYTES),
        cost_estimate=pl.CostEstimate(
            flops=4 * coords * spans * SPAN * corners * row_count * width,
            bytes_accessed=4 * (met.size + diag.size + face.size),
            transcendentals=0,
        ),
        name="cells_and_nodes",
    )(adj, fringe_cell[0], node_id[0], met, diag, face)

    received = lax.all_to_all(sent, ("dom", "grid"), split_axis=0, concat_axis=0, tiled=True)
    from_below = shifted(down, "dom", -1)
    from_above = shifted(up, "dom", 1)

    minus_weight, held = pl.pallas_call(
        prepare,
        in_specs=[smem] + [vmem] * 2,
        out_specs=[vmem] * 2,
        out_shape=[
            jax.ShapeDtypeStruct((peers, width), jnp.float32),
            jax.ShapeDtypeStruct((variables, row_count, width), jnp.float32),
        ],
        compiler_params=pltpu.CompilerParams(vmem_limit_bytes=20 * 1024 * 1024),
        cost_estimate=pl.CostEstimate(flops=base.size, bytes_accessed=8 * base.size, transcendentals=0),
        name="prepare",
    )(donor_count, fringe_weight[0], base)

    product, node_sens = pl.pallas_call(
        finish,
        in_specs=[vmem] * 6,
        out_specs=[vmem] * 2,
        out_shape=[
            jax.ShapeDtypeStruct((variables, row_count, width), jnp.float32),
            jax.ShapeDtypeStruct((coords, NODE_DEV), jnp.float32),
        ],
        compiler_params=pltpu.CompilerParams(vmem_limit_bytes=20 * 1024 * 1024),
        name="finish",
    )(received, from_below, from_above, donor_cell[0], minus_weight, held)
    return (product[None], node_sens)


def solution(mesh):
    in_specs = (
        P("grid", None, "dom", None),
        P("grid", None, None, "dom", None),
        P("grid", None, None, None, "dom", None),
        P("grid", None, None, None, "dom", None),
        P("grid", None, "dom", None),
        P(("dom", "grid"), None, None),
        P(("dom", "grid"), None, None),
        P(("dom", "grid"), None, None),
        P(("dom", "grid"), None),
    )
    out_specs = (P("grid", None, "dom", None), P(None, ("dom", "grid")))
    return jax.shard_map(local, mesh=mesh, in_specs=in_specs, out_specs=out_specs, check_vma=False)
```
